32 devices in a mesh: ctx: 4 (over x, core), tp: 8 (over z, y).
Axes of the slice: x: 2, y: 2, z: 4, core: 2. Of those that a mesh axis runs over, the one named last changes fastest.
Arguments:
- streams: bfloat16 [3, 4096, 8192], P(None, 'ctx', 'tp'), may hold values from -6 to 6
- conv_weight: float32 [3, 3, 8192], P(None, None, 'tp'), may hold values from -3.5 to 3.5
- skip_weight: float32 [8192], P('tp'), may hold values from -4 to 4
- long_filter: bfloat16 [4096, 8192], P('ctx', 'tp'), may hold values from -1.6 to 1.6
- out_weight: bfloat16 [8192, 8192], P('tp'), may hold values from -0.09375 to 0.09375
Outputs:
- projected: bfloat16 [4096, 8192], P('ctx', 'tp')
The draws below stay inside these ranges and needn't reach their ends.
All inputs are finite; a program needn't handle non-finite values.
Results may differ from the reference program's by a relative error of at most 0.015.
Values may be sent and summed in bfloat16 or wider, within the bound.
No kernel may reach another device: no remote copies, remote signals or barrier semaphores. Data moves between devices by JAX's collectives and lax.ppermute only.
A program may use at most 192 MiB of HBM per device.

```python
import jax
import jax.numpy as jnp
from jax import lax

D = 8192
KCONV = 3
SEQUENCE_LENGTH = 4096


def draw_long_filter(key, part):
    gradual_decay_key, decay_rate_key, quick_decay_key, spike_key, jitter_key = jax.random.split(jax.random.fold_in(key, 7101), 5)
    slow_share = 0.5
    slow_pick = jax.random.bernoulli(gradual_decay_key, slow_share, (D,))
    slow_rate = jnp.exp(jax.random.uniform(decay_rate_key, (D,), jnp.float32, jnp.log(0.25 / SEQUENCE_LENGTH), jnp.log(2.0 / SEQUENCE_LENGTH)))
    fast_rate = jnp.exp(jax.random.uniform(quick_decay_key, (D,), jnp.float32, jnp.log(1.0 / 50.0), jnp.log(1.0 / 20.0)))
    decay_rates = jnp.where(slow_pick, slow_rate, fast_rate)
    spike_events = jax.random.randint(spike_key, (3,), 1, SEQUENCE_LENGTH)
    offset_steps = jnp.arange(SEQUENCE_LENGTH, dtype=jnp.int32)
    returned_filter = (offset_steps[:, None] >= spike_events[None, :]).astype(jnp.float32)
    spike_multiplier = jnp.exp(jnp.log(0.6) * (returned_filter[:, 0] + returned_filter[:, 1] + returned_filter[:, 2]))
    decay_profile = jnp.exp(-decay_rates[None, :] * offset_steps.astype(jnp.float32)[:, None]) * spike_multiplier[:, None]
    scale_sq = (1.0 - jnp.exp(-2.0 * decay_rates * SEQUENCE_LENGTH)) / (1.0 - jnp.exp(-2.0 * decay_rates))
    noise = jnp.clip(jax.random.normal(jitter_key, (SEQUENCE_LENGTH, D), jnp.float32), -5.0, 5.0)
    return (noise * decay_profile / jnp.sqrt(scale_sq)[None, :]).astype(jnp.bfloat16)


def with_spikes(array, own_key, source, target, blocks, factor):
    owner, partner = [(jnp.arange(array.shape[position]) // (array.shape[position] // blocks)).reshape([-1 if axis == position else 1 for axis in range(array.ndim)]) for position in (source, target)]
    chosen = jax.random.permutation(own_key, blocks)[partner]
    strong = (owner == chosen) | (owner == (partner + blocks // 2) % blocks)
    return jnp.where(strong, factor * array, array)


def block_levels(key, dims, cuts, least, top_value):
    level, own = 1.0, jax.random.fold_in(key, 6)
    for position, parts in cuts:
        draws = jnp.exp(jax.random.uniform(jax.random.fold_in(own, position), (parts,), jnp.float32, least / len(cuts), top_value / len(cuts)))
        level = level * jnp.repeat(draws, dims[position] // parts).reshape([-1 if axis == position else 1 for axis in range(len(dims))])
    return level


def centred(rng, extent, width, reach, cuts=(), kind=jnp.bfloat16):
    entries = jax.random.normal(rng, extent, jnp.float32) * width
    if len(cuts) > 0:
        entries = block_levels(rng, extent, cuts, -0.22, 0.18) * entries
    return jnp.clip(entries, min=-reach, max=reach).astype(kind)


def bell_draw_with(rng, dims, scale, limit, cuts, heavy, kind=jnp.bfloat16):
    drawn = scale * jax.random.normal(rng, dims, jnp.float32)
    if cuts:
        drawn = drawn * block_levels(rng, dims, cuts, -0.22, 0.18)
    return jnp.clip(with_spikes(drawn, jax.random.fold_in(rng, 3), *heavy), -limit, limit).astype(kind)


def setup_inputs(seed: int = 0) -> dict:
    splits = jax.random.split(jax.random.key(seed), 6)
    streams = centred(splits[0], (3, SEQUENCE_LENGTH, D), 1.0, 6.0, ((1, 4), (2, 8)))
    conv_weight = centred(splits[1], (3, KCONV, D), KCONV ** -0.5, 3.5, ((2, 8),), jnp.float32)
    skip_weight = centred(splits[2], (D,), 1.0, 4.0, ((0, 8),), jnp.float32)
    long_filter = draw_long_filter(jax.random.fold_in(splits[5], 71), 0)
    out_weight = bell_draw_with(splits[4], (D, D), D ** -0.5, 0.09375, ((0, 8),), (0, 1, 8, 2.0))
    return dict(streams=streams, conv_weight=conv_weight, skip_weight=skip_weight, long_filter=long_filter, out_weight=out_weight)


def short_conv(streams, conv_weight):
    values = streams.astype(jnp.float32)
    padded = jnp.pad(values, ((0, 0), (KCONV - 1, 0), (0, 0)))
    summed = jnp.zeros(values.shape, jnp.float32)
    for lag_step in range(KCONV):
        begin = KCONV - 1 - lag_step
        summed = summed + conv_weight[:, lag_step, None, :].astype(jnp.float32) * padded[:, begin:begin + SEQUENCE_LENGTH, :]
    return summed


def long_conv(mixed_u, long_filter):
    block_width = min(D, 512)
    block_count = D // block_width
    signal = mixed_u.astype(jnp.float32).reshape(SEQUENCE_LENGTH, block_count, block_width).transpose(1, 0, 2)
    kernel = long_filter.astype(jnp.float32).reshape(SEQUENCE_LENGTH, block_count, block_width).transpose(1, 0, 2)

    def one_block(pair):
        sig_block, ker_block = pair
        spec_sig = jnp.fft.rfft(sig_block, n=2 * SEQUENCE_LENGTH, axis=0)
        spec_ker = jnp.fft.rfft(ker_block, n=2 * SEQUENCE_LENGTH, axis=0)
        return jnp.fft.irfft(spec_sig * spec_ker, n=2 * SEQUENCE_LENGTH, axis=0)[:SEQUENCE_LENGTH]

    result = lax.map(one_block, (signal, kernel))
    return result.transpose(1, 0, 2).reshape(SEQUENCE_LENGTH, D)


def reference(streams, conv_weight, skip_weight, long_filter, out_weight):
    conv_out = short_conv(streams, conv_weight)
    gating = conv_out[0]
    mixed_u = (conv_out[1] * conv_out[2]).astype(jnp.bfloat16)
    long_out = long_conv(mixed_u, long_filter).astype(jnp.bfloat16)
    gated = ((long_out.astype(jnp.float32) + skip_weight[None, :] * mixed_u.astype(jnp.float32)) * gating).astype(jnp.bfloat16)
    return jnp.dot(gated, out_weight, preferred_element_type=jnp.float32).astype(jnp.bfloat16)
```

```python
import math

import jax
import jax.numpy as jnp
from jax import lax
from jax.sharding import PartitionSpec as P

three_pass = lax.Precision.HIGH


def shifted(value, axis, steps):
    count = lax.axis_size(axis)
    initial, last = (max(0, -steps), min(count, count - steps))
    return lax.ppermute(value, axis, [(source, source + steps) for source in range(initial, last)])


def fft_conv(signal, kernel):
    seq_len, chan_count = signal.shape
    full_len = 2 * seq_len
    col_count = 128
    row_count = full_len // col_count
    half_rows = row_count // 2
    row_index = lax.iota(jnp.int32, row_count)
    half_index = lax.iota(jnp.int32, half_rows)
    col_index = lax.iota(jnp.int32, col_count)
    angle_rows = (row_index[:, None] * half_index[None, :] % row_count).astype(jnp.float32) * (
        2.0 * math.pi / row_count
    )
    cos_rows = jnp.cos(angle_rows)
    sin_rows = jnp.sin(angle_rows)
    angle_twist = (row_index[:, None] * col_index[None, :] % full_len).astype(jnp.float32) * (
        2.0 * math.pi / full_len
    )
    cos_twist = jnp.cos(angle_twist)
    sin_twist = jnp.sin(angle_twist)
    angle_cols = (col_index[:, None] * col_index[None, :] % col_count).astype(jnp.float32) * (
        2.0 * math.pi / col_count
    )
    cos_cols = jnp.cos(angle_cols)
    sin_cols = jnp.sin(angle_cols)

    def forward(field):
        re_first = jnp.einsum("an,cnm->cam", cos_rows, field, precision=three_pass)
        im_first = -jnp.einsum("an,cnm->cam", sin_rows, field, precision=three_pass)
        re_twist = re_first * cos_twist + im_first * sin_twist
        im_twist = im_first * cos_twist - re_first * sin_twist
        re_spec = jnp.einsum("cam,mk->cak", re_twist, cos_cols, precision=three_pass) + jnp.einsum(
            "cam,mk->cak", im_twist, sin_cols, precision=three_pass
        )
        im_spec = jnp.einsum("cam,mk->cak", im_twist, cos_cols, precision=three_pass) - jnp.einsum(
            "cam,mk->cak", re_twist, sin_cols, precision=three_pass
        )
        return (re_spec, im_spec)

    sig_field = signal.astype(jnp.float32).T.reshape(chan_count, half_rows, col_count)
    ker_field = kernel.astype(jnp.float32).T.reshape(chan_count, half_rows, col_count)
    re_sig, im_sig = forward(sig_field)
    re_ker, im_ker = forward(ker_field)
    re_prod = re_sig * re_ker - im_sig * im_ker
    im_prod = re_sig * im_ker + im_sig * re_ker
    re_back = jnp.einsum("cak,mk->cam", re_prod, cos_cols, precision=three_pass) - jnp.einsum(
        "cak,mk->cam", im_prod, sin_cols, precision=three_pass
    )
    im_back = jnp.einsum("cak,mk->cam", im_prod, cos_cols, precision=three_pass) + jnp.einsum(
        "cak,mk->cam", re_prod, sin_cols, precision=three_pass
    )
    re_untwist = re_back * cos_twist - im_back * sin_twist
    im_untwist = im_back * cos_twist + re_back * sin_twist
    output_field = jnp.einsum(
        "an,cam->cnm", cos_rows, re_untwist, precision=three_pass
    ) - jnp.einsum("an,cam->cnm", sin_rows, im_untwist, precision=three_pass)
    output_field = output_field * (1.0 / full_len)
    return output_field.reshape(chan_count, seq_len).T


def swapped(value, axis, bits):
    count = lax.axis_size(axis)
    return lax.ppermute(value, axis, [(source, source ^ bits) for source in range(count)])


def column_block(weights, block, width):
    return lax.dynamic_slice_in_dim(weights, block * width, width, axis=1)


def swapped_weights(out_weight):
    count = lax.axis_size("tp")
    me = lax.axis_index("tp")
    core = lax.rem(lax.axis_index("ctx"), 2)
    rows, width = (out_weight.shape[0], out_weight.shape[1] // count)
    half = rows // 2
    blocks = {}
    for high in range(count // 4):
        for low in range(2):
            wanted = me ^ (4 * high + low)
            own = column_block(out_weight, wanted, width)
            part = lax.dynamic_slice(out_weight, (core * half, (wanted ^ 2) * width), (half, width))
            direct = swapped(part, "tp", 2)
            shared = swapped(direct, "ctx", 1)
            first = jnp.where(core == 0, direct, shared)
            second = jnp.where(core == 0, shared, direct)
            blocks[high, low] = (own, jnp.concatenate([first, second], axis=0))
    return blocks


def project(gated, blocks):
    high_count = lax.axis_size("tp") // 4
    pieces = 2
    step = gated.shape[0] // pieces
    results = []
    for piece in range(pieces):
        near = gated[piece * step : (piece + 1) * step]
        far = swapped(near, "tp", 2)

        def partial_sum(high, low):
            own, other = blocks[high, low]
            return jnp.dot(near, own, preferred_element_type=jnp.float32) + jnp.dot(
                far, other, preferred_element_type=jnp.float32
            )

        arrived = []
        for high in reversed(range(high_count)):
            sent = swapped(partial_sum(high, 1).astype(jnp.bfloat16), "tp", 1)
            total = partial_sum(high, 0) + sent.astype(jnp.float32)
            if high:
                arrived.append(swapped(total.astype(jnp.bfloat16), "tp", 4 * high))
        for value in arrived:
            total = total + value.astype(jnp.float32)
        results.append(total.astype(jnp.bfloat16))
    return jnp.concatenate(results, axis=0)


def on_device(streams, conv_weight, skip_weight, long_filter, out_weight):
    tok_rows = streams.shape[1]
    chan_cols = streams.shape[2]
    tap_count = conv_weight.shape[1]
    rim_rows = shifted(streams[:, tok_rows - (tap_count - 1) :, :], "ctx", 1)
    extended = jnp.concatenate([rim_rows, streams], axis=1).astype(jnp.float32)
    summed = jnp.zeros((3, tok_rows, chan_cols), jnp.float32)
    for lag_step in range(tap_count):
        begin = tap_count - 1 - lag_step
        summed = (
            summed + conv_weight[:, lag_step, None, :] * extended[:, begin : begin + tok_rows, :]
        )
    gating = summed[0]
    mixed_u = (summed[1] * summed[2]).astype(jnp.bfloat16)
    groups = lax.axis_size("ctx")
    group_width = chan_cols // groups
    mixed_three = mixed_u.reshape(tok_rows, groups, group_width)
    filter_three = long_filter.reshape(tok_rows, groups, group_width)
    signal_full = lax.all_to_all(mixed_three, "ctx", split_axis=1, concat_axis=0, tiled=True)
    kernel_full = lax.all_to_all(filter_three, "ctx", split_axis=1, concat_axis=0, tiled=True)
    long_part = fft_conv(signal_full[:, 0, :], kernel_full[:, 0, :]).astype(jnp.bfloat16)[
        :, None, :
    ]
    long_three = lax.all_to_all(long_part, "ctx", split_axis=0, concat_axis=1, tiled=True)
    long_out = long_three.reshape(tok_rows, chan_cols)
    gated = (
        (long_out.astype(jnp.float32) + skip_weight[None, :] * mixed_u.astype(jnp.float32)) * gating
    ).astype(jnp.bfloat16)
    return project(gated, swapped_weights(out_weight))


def solution(mesh):
    return jax.shard_map(
        on_device,
        mesh=mesh,
        in_specs=(
            P(None, "ctx", "tp"),
            P(None, None, "tp"),
            P("tp"),
            P("ctx", "tp"),
            P("tp", None),
        ),
        out_specs=P("ctx", "tp"),
        check_vma=False,
    )
```

```python
import functools

import jax
import jax.numpy as jnp
import ml_dtypes
import numpy as np
from jax import lax
from jax.experimental import pallas as pl
from jax.experimental.pallas import tpu as pltpu
from jax.sharding import PartitionSpec as P

LANES = 128
PART = 16
SPARE = 8
VMEM_BYTES = 48 << 20


def swapped(value, axis, bits):
    count = lax.axis_size(axis)
    return lax.ppermute(value, axis, [(source, source ^ bits) for source in range(count)])


def shifted(value, axis, steps):
    count = lax.axis_size(axis)
    initial, last = (max(0, -steps), min(count, count - steps))
    return lax.ppermute(value, axis, [(source, source + steps) for source in range(initial, last)])


def after(value, *others):
    return lax.optimization_barrier((value, *others))[0]


def exchanged(pieces):
    return [pieces[0]] + [swapped(pieces[p], "ctx", p) for p in range(1, len(pieces))]


def tables(rows, cols, groups):
    half = rows // 2
    total = rows * cols
    slow, freq = np.arange(half), np.arange(half + 1)
    angle = 2 * np.pi * (freq[:, None] * slow[None, :] % rows) / rows
    first = np.concatenate([np.cos(angle), -np.sin(angle)[1:half]], 0)
    weight = np.where((freq == 0) | (freq == half), 1.0, 2.0)[:, None] / total
    last = np.concatenate([np.cos(angle) * weight, -(np.sin(angle) * weight)[1:half]], 0).T
    order = (np.arange(groups)[:, None] ^ np.arange(groups)[None, :])[:, :, None] * (half // groups)
    order = (order + np.arange(half // groups)).reshape(groups, half)
    col = np.arange(cols)
    turn = rows * col[None, :, None] * col[None, None, :]
    angle = 2 * np.pi * ((freq[:, None, None] * col[None, None, :] + turn) % total) / total
    cosine, sine = np.cos(angle), np.sin(angle)
    middle = np.concatenate(
        [np.concatenate([cosine, sine], 2), np.concatenate([-sine, cosine], 2)], 1
    )

    def pair(value):
        high = value.astype(ml_dtypes.bfloat16)
        low = (value - high.astype(np.float64)).astype(ml_dtypes.bfloat16)
        return np.concatenate([high, low], -1)

    first_all = np.stack([pair(first[:, own]) for own in order])
    last_all = np.stack([pair(last[own]) for own in order])
    return first_all, pair(middle), pair(middle.transpose(0, 2, 1)), last_all


def dot(left, right):
    return jnp.dot(left, right, preferred_element_type=jnp.float32)


def product(table, value):
    high = value.astype(jnp.bfloat16)
    low = (value - high.astype(jnp.float32)).astype(jnp.bfloat16)
    return dot(
        jnp.concatenate([table, table], axis=1), jnp.concatenate([high, high, low, low], axis=0)
    )


def conv_kernel(groups, me_ref, first_ref, mid_ref, back_ref, last_ref, *refs):
    signal, kernel, out = refs[:groups], refs[groups : 2 * groups], refs[2 * groups : 3 * groups]
    spec_signal, spec_kernel, mixed = refs[3 * groups :]
    cols, part, width = signal[0].shape
    rows = first_ref.shape[0]
    half = rows // 2
    pitch, pitch_back = cols_pitch(spec_signal, cols), cols_pitch(mixed, rows)

    def forward(col, carry):
        field = jnp.concatenate(
            [jnp.concatenate([ref[col] for ref in source], axis=0) for source in (signal, kernel)],
            axis=1,
        )
        spec = dot(first_ref[...], jnp.concatenate([field, field], axis=0))
        place = pl.ds(pl.multiple_of(col * pitch, 8), rows)
        spec_signal[place, :] = spec[:, :width]
        spec_kernel[place, :] = spec[:, width:]
        return carry

    def middle(freq, edge):
        def take(row):
            place = pl.ds(row, cols, stride=pitch)
            return jnp.concatenate([spec_signal[place, :], spec_kernel[place, :]], axis=1)

        real = take(freq)
        imag = jnp.zeros_like(real) if edge else take(freq + half)
        spec = product(mid_ref[freq], jnp.concatenate([real, imag], axis=0))
        re_sig, im_sig = spec[:cols, :width], spec[cols:, :width]
        re_ker, im_ker = spec[:cols, width:], spec[cols:, width:]
        both = jnp.concatenate(
            [re_sig * re_ker - im_sig * im_ker, re_sig * im_ker + im_sig * re_ker], axis=0
        )
        field = product(back_ref[freq], both)
        mixed[pl.ds(pl.multiple_of(freq * pitch_back, 8), cols), :] = field[:cols]
        if not edge:
            place = pl.ds(pl.multiple_of((freq + half) * pitch_back, 8), cols)
            mixed[place, :] = field[cols:]

    def inner(freq, carry):
        middle(freq, False)
        return carry

    def backward(col, carry):
        field = mixed[pl.ds(col, rows, stride=pitch_back), :]
        result = product(last_ref[...], field).astype(jnp.bfloat16)
        for group in range(groups):
            out[group][col] = result[group * part : (group + 1) * part]
        return carry

    lax.fori_loop(0, cols, forward, 0, unroll=16)
    middle(0, True)
    middle(half, True)
    lax.fori_loop(1, half, inner, 0, unroll=9 if (half - 1) % 9 == 0 else 1)
    lax.fori_loop(0, cols, backward, 0, unroll=16)


def cols_pitch(ref, count):
    return ref.shape[0] // count


def whole(shape):
    return pl.BlockSpec(shape, lambda *_: (0,) * len(shape))


def long_conv(me, signal, kernel):
    groups = len(signal)
    cols, part, width = signal[0].shape
    rows = 2 * groups * part
    first, mid, back, last = tables(rows, cols, groups)
    flops = 2 * width * (4 * rows * cols * rows + 12 * (rows // 2 + 1) * 4 * cols * cols)
    return pl.pallas_call(
        functools.partial(conv_kernel, groups),
        grid_spec=pltpu.PrefetchScalarGridSpec(
            num_scalar_prefetch=1,
            grid=(1,),
            in_specs=[
                pl.BlockSpec((None, *first.shape[1:]), lambda _, me: (me[0], 0, 0)),
                whole(mid.shape),
                whole(back.shape),
                pl.BlockSpec((None, *last.shape[1:]), lambda _, me: (me[0], 0, 0)),
            ]
            + [whole(signal[0].shape)] * (2 * groups),
            out_specs=[whole(signal[0].shape)] * groups,
            scratch_shapes=[pltpu.VMEM((cols * (rows + SPARE), width), jnp.float32)] * 2
            + [pltpu.VMEM((rows * (cols + SPARE), width), jnp.float32)],
        ),
        out_shape=[jax.ShapeDtypeStruct(signal[0].shape, jnp.bfloat16)] * groups,
        compiler_params=pltpu.CompilerParams(vmem_limit_bytes=VMEM_BYTES),
        cost_estimate=pl.CostEstimate(
            flops=flops, bytes_accessed=mid.nbytes * 2 + 12 * signal[0].size, transcendentals=0
        ),
        name="long_conv",
    )(me, first, mid, back, last, *signal, *kernel)


def spread(value, natural, out):
    cols, part, _ = out.shape
    pitch = cols + SPARE
    for slow in range(part):
        natural[slow * pitch : slow * pitch + cols, :] = value(slow * cols, cols)
    for col in range(cols):
        out[col] = natural[pl.ds(col, part, stride=pitch), :].astype(jnp.bfloat16)


def short_conv(buffer, stream, rim_ref, data_ref, taps_ref):
    count = data_ref.shape[0]
    taps = taps_ref.shape[1]
    buffer[SPARE - (taps - 1) : SPARE, :] = rim_ref[stream].astype(jnp.float32)
    buffer[SPARE : SPARE + count, :] = data_ref[...].astype(jnp.float32)

    def rows(begin, size):
        total = None
        for lag in range(taps):
            place = slice(SPARE + begin - lag, SPARE + begin - lag + size)
            term = taps_ref[stream, lag : lag + 1, :] * buffer[place, :]
            total = term if total is None else total + term
        return total

    return rows


def filter_kernel(groups, me_ref, data_ref, *refs):
    out, natural = refs[:groups], refs[groups]
    for group in range(groups):

        @pl.when(pl.program_id(0) == group)
        def _(group=group):
            spread(
                lambda begin, size: data_ref[begin : begin + size, :].astype(jnp.float32),
                natural,
                out[group],
            )


def mixed_kernel(groups, me_ref, key_ref, value_ref, rim_ref, taps_ref, *refs):
    out, (natural, key_rows, value_rows) = refs[:groups], refs[groups:]
    key = short_conv(key_rows, 1, rim_ref, key_ref, taps_ref)
    value = short_conv(value_rows, 2, rim_ref, value_ref, taps_ref)
    for group in range(groups):

        @pl.when(pl.program_id(0) == group)
        def _(group=group):
            spread(
                lambda begin, size: key(begin, size) * value(begin, size), natural, out[group]
            )


def gate_kernel(gate_ref, key_ref, value_ref, rim_ref, taps_ref, skip_ref, gating_ref, direct_ref, *rows):
    convs = [
        short_conv(buffer, stream, rim_ref, data, taps_ref)
        for stream, (buffer, data) in enumerate(zip(rows, (gate_ref, key_ref, value_ref)))
    ]
    step = 128
    for begin in range(0, gate_ref.shape[0], step):
        gating, key, value = (conv(begin, step) for conv in convs)
        mixed = (key * value).astype(jnp.bfloat16).astype(jnp.float32)
        gating_ref[begin : begin + step, :] = gating
        direct_ref[begin : begin + step, :] = skip_ref[...] * mixed


def gated_kernel(groups, me_ref, gating_ref, direct_ref, *refs):
    parts, (out, natural) = refs[:groups], refs[groups:]
    cols, part, _ = parts[0].shape
    pitch = cols + SPARE
    for group in range(groups):

        @pl.when(pl.program_id(0) == group)
        def _(group=group):
            for col in range(cols):
                natural[pl.ds(col, part, stride=pitch), :] = parts[group][col].astype(jnp.float32)

    for slow in range(part):
        place = slice(slow * cols, (slow + 1) * cols)
        long = natural[slow * pitch : slow * pitch + cols, :]
        out[place, :] = ((long + direct_ref[place, :]) * gating_ref[place, :]).astype(jnp.bfloat16)


def in_groups(kernel, groups, chunk, me, specs, out_specs, out_shape, scratch, name, *args):
    return pl.pallas_call(
        kernel,
        grid_spec=pltpu.PrefetchScalarGridSpec(
            num_scalar_prefetch=1,
            grid=(groups,),
            in_specs=specs,
            out_specs=out_specs,
            scratch_shapes=scratch,
        ),
        out_shape=out_shape,
        compiler_params=pltpu.CompilerParams(vmem_limit_bytes=VMEM_BYTES),
        name=name,
    )(me, *args)


class Chunk:
    def __init__(self, index, groups, tokens, me):
        self.groups, self.tokens, self.me = groups, tokens, me
        self.cols = tokens // PART
        self.piece = (self.cols, PART, LANES)
        self.block = lambda step, me: index * groups + (me[0] ^ step)
        self.index = index

    def column(self, *lead):
        sizes, places = zip(*lead)
        return pl.BlockSpec(
            (*sizes, LANES), lambda step, me: (*places, self.block(step, me))
        )

    def call(self, kernel, specs, out_specs, out_shape, scratch, name, *args):
        return in_groups(
            functools.partial(kernel, self.groups), self.groups, self.index, self.me,
            specs, out_specs, out_shape, scratch, name, *args,
        )

    def natural(self):
        return pltpu.VMEM((PART * (self.cols + SPARE), LANES), jnp.float32)

    def rows(self):
        return pltpu.VMEM((SPARE + self.tokens, LANES), jnp.float32)

    def pieces(self):
        shape = jax.ShapeDtypeStruct(self.piece, jnp.bfloat16)
        return [whole(self.piece)] * self.groups, [shape] * self.groups

    def filter_pieces(self, long_filter):
        return self.call(
            filter_kernel, [self.column((self.tokens, 0))], *self.pieces(),
            [self.natural()], "filter_pieces", long_filter,
        )

    def mixed_pieces(self, streams, rim, taps):
        specs = [self.column((None, 1), (self.tokens, 0)), self.column((None, 2), (self.tokens, 0))]
        return self.call(
            mixed_kernel, specs + self.small(rim, taps), *self.pieces(),
            [self.natural(), self.rows(), self.rows()], "mixed_pieces", streams, streams, rim, taps,
        )

    def small(self, rim, taps):
        return [
            self.column((rim.shape[0], 0), (rim.shape[1], 0)),
            self.column((taps.shape[0], 0), (taps.shape[1], 0)),
        ]

    def gates(self, streams, rim, taps, skip):
        specs = [self.column((None, stream), (self.tokens, 0)) for stream in range(3)]
        specs += self.small(rim, taps) + [self.column((1, 0))]
        spec = pl.BlockSpec((self.tokens, LANES), lambda step, me: (0, me[0] ^ step))
        shape = jax.ShapeDtypeStruct((self.tokens, self.groups * LANES), jnp.float32)

        def kernel(groups, me_ref, *refs):
            gate_kernel(*refs)

        return self.call(
            kernel, specs, [spec] * 2, [shape] * 2, [self.rows()] * 3, "gates",
            streams, streams, streams, rim, taps, skip,
        )

    def gated(self, gating, direct, parts):
        spec = pl.BlockSpec((self.tokens, LANES), lambda step, me: (0, me[0] ^ step))
        shape = jax.ShapeDtypeStruct((self.tokens, self.groups * LANES), jnp.bfloat16)
        return self.call(
            gated_kernel, [spec] * 2 + [whole(self.piece)] * self.groups, spec, shape,
            [self.natural()], "gated", gating, direct, *parts,
        )


def swapped_weights(out_weight, chunks):
    count = lax.axis_size("tp")
    me = lax.axis_index("tp")
    core = lax.rem(lax.axis_index("ctx"), 2)
    rows, width = (out_weight.shape[0], out_weight.shape[1] // count)
    half = rows // 2
    blocks = {}
    for high in reversed(range(count // 4)):
        for low in reversed(range(2)):
            wanted = me ^ (4 * high + low)
            own = lax.dynamic_slice_in_dim(out_weight, wanted * width, width, axis=1)
            part = lax.dynamic_slice(out_weight, (core * half, (wanted ^ 2) * width), (half, width))
            direct = swapped(part, "tp", 2)
            shared = swapped(direct, "ctx", 1)
            first = jnp.where(core == 0, direct, shared)
            second = jnp.where(core == 0, shared, direct)
            far = [first, second] if chunks == 2 else [jnp.concatenate([first, second], axis=0)]
            blocks[high, low] = ([own[i * (rows // chunks) : (i + 1) * (rows // chunks)] for i in range(chunks)], far)
    return blocks


def project(gated, blocks, pieces):
    high_count = lax.axis_size("tp") // 4
    step = gated[0].shape[0] // pieces
    results = []
    for piece in range(pieces):
        near = [chunk[piece * step : (piece + 1) * step] for chunk in gated]
        far = [swapped(chunk, "tp", 2) for chunk in near]

        def partial_sum(high, low):
            own, other = blocks[high, low]
            total = None
            for value, weight in zip(near + far, own + other):
                term = dot(value, weight)
                total = term if total is None else total + term
            return total

        arrived = []
        for high in reversed(range(high_count)):
            sent = swapped(partial_sum(high, 1).astype(jnp.bfloat16), "tp", 1)
            total = partial_sum(high, 0) + sent.astype(jnp.float32)
            if high:
                arrived.append(swapped(total.astype(jnp.bfloat16), "tp", 4 * high))
        for value in arrived:
            total = total + value.astype(jnp.float32)
        results.append(total.astype(jnp.bfloat16))
    return jnp.concatenate(results, axis=0)


def widened(value, groups):
    group = value.shape[-1] // groups
    if group >= LANES:
        return value
    split = value.reshape(*value.shape[:-1], groups, group)
    padded = jnp.pad(split, [(0, 0)] * (split.ndim - 1) + [(0, LANES - group)])
    return padded.reshape(*value.shape[:-1], groups * LANES)


def on_device(streams, conv_weight, skip_weight, long_filter, out_weight):
    tokens, channels = streams.shape[1:]
    taps = conv_weight.shape[1]
    groups = lax.axis_size("ctx")
    me = lax.axis_index("ctx").astype(jnp.int32).reshape(1)
    group = channels // groups
    streams, conv_weight, skip_weight, long_filter = (
        widened(value, groups) for value in (streams, conv_weight, skip_weight[None], long_filter)
    )
    chunks = streams.shape[2] // (groups * LANES)
    rim = shifted(streams[:, tokens - (taps - 1) :, :], "ctx", 1)
    parts = [Chunk(index, groups, tokens, me) for index in range(chunks)]
    arrived = []
    before = ()
    for part in parts:
        filters = part.filter_pieces(after(long_filter, *before))
        mixed = part.mixed_pieces(streams, after(rim, filters[0]), conv_weight)
        arrived.append((exchanged(mixed), exchanged(filters)))
        before = (mixed[0],)
    blocks = swapped_weights(after(out_weight, *before), chunks)
    gates = [part.gates(streams, after(rim, *before), conv_weight, skip_weight) for part in parts]
    gated = []
    for part, (signal, kernel), (gating, direct) in zip(parts, arrived, gates):
        result = exchanged(long_conv(me, signal, kernel))
        value = part.gated(gating, direct, result)
        if group < LANES:
            value = value.reshape(tokens, groups, LANES)[:, :, :group].reshape(tokens, channels)
        gated.append(value)
    return project(gated, blocks, PIECES)


PIECES = 4


def solution(mesh):
    return jax.shard_map(
        on_device,
        mesh=mesh,
        in_specs=(
            P(None, "ctx", "tp"),
            P(None, None, "tp"),
            P("tp"),
            P("ctx", "tp"),
            P("tp", None),
        ),
        out_specs=P("ctx", "tp"),
        check_vma=False,
    )
```

```python
import functools

import jax
import jax.numpy as jnp
import ml_dtypes
import numpy as np
from jax import lax
from jax.experimental import pallas as pl
from jax.experimental.pallas import tpu as pltpu
from jax.sharding import PartitionSpec as P

LANES = 128
PART = 16
SPARE = 8
VMEM_BYTES = 48 << 20
SHORT = pl.CostEstimate(flops=1, bytes_accessed=1, transcendentals=0)


def swapped(value, axis, bits):
    count = lax.axis_size(axis)
    return lax.ppermute(value, axis, [(source, source ^ bits) for source in range(count)])


def shifted(value, axis, steps):
    count = lax.axis_size(axis)
    initial, last = (max(0, -steps), min(count, count - steps))
    return lax.ppermute(value, axis, [(source, source + steps) for source in range(initial, last)])


def after(value, *others):
    return lax.optimization_barrier((value, *others))[0]


def exchanged(low, high, *others):
    half = low.shape[0]
    high = after(swapped(high, "ctx", half), *others)
    slots = [(low, place) for place in range(half)] + [(high, place) for place in range(half)]
    bit = half // 2
    while bit:
        moving = [slot for slot in range(2 * half) if slot & bit]
        sent = jnp.stack([slots[slot][0][slots[slot][1]] for slot in moving])
        arrived = swapped(sent, "ctx", bit)
        for place, slot in enumerate(moving):
            slots[slot] = (arrived, place)
        bit //= 2
    return slots


def slot_spec(slot):
    array, place = slot
    return pl.BlockSpec((None, *array.shape[1:]), lambda *_: (place,) + (0,) * (array.ndim - 1))


def slot_ref(halves, slot):
    count = halves[0].shape[0]
    return halves[slot // count].at[slot % count]


def tied(slots, *others):
    array, place = slots[0]
    return [(after(array, *others), place)] + slots[1:]


def tables(rows, cols, groups):
    half = rows // 2
    total = rows * cols
    slow, freq = np.arange(half), np.arange(half + 1)
    angle = 2 * np.pi * (freq[:, None] * slow[None, :] % rows) / rows
    first = np.concatenate([np.cos(angle), -np.sin(angle)[1:half]], 0)
    weight = np.where((freq == 0) | (freq == half), 1.0, 2.0)[:, None] / total
    last = np.concatenate([np.cos(angle) * weight, -(np.sin(angle) * weight)[1:half]], 0).T
    order = (np.arange(groups)[:, None] ^ np.arange(groups)[None, :])[:, :, None] * (half // groups)
    order = (order + np.arange(half // groups)).reshape(groups, half)
    col = np.arange(cols)
    turn = rows * col[None, :, None] * col[None, None, :]
    angle = 2 * np.pi * ((freq[:, None, None] * col[None, None, :] + turn) % total) / total
    cosine, sine = np.cos(angle), np.sin(angle)
    middle = np.concatenate(
        [np.concatenate([cosine, sine], 2), np.concatenate([-sine, cosine], 2)], 1
    )

    def pair(value):
        high = value.astype(ml_dtypes.bfloat16)
        low = (value - high.astype(np.float64)).astype(ml_dtypes.bfloat16)
        return np.concatenate([high, low], -1)

    first_all = np.stack([pair(first[:, own]) for own in order])
    last_all = np.stack([pair(last[own]) for own in order])
    return first_all, pair(middle), pair(middle.transpose(0, 2, 1)), last_all


def dot(left, right):
    return jnp.dot(left, right, preferred_element_type=jnp.float32)


def product(table, value):
    high = value.astype(jnp.bfloat16)
    low = (value - high.astype(jnp.float32)).astype(jnp.bfloat16)
    return dot(
        jnp.concatenate([table, table], axis=1), jnp.concatenate([high, high, low, low], axis=0)
    )


def conv_kernel(groups, me_ref, first_ref, mid_ref, back_ref, last_ref, *refs):
    fields, out = refs[:groups], refs[groups : groups + 2]
    spec_signal, spec_kernel, mixed = refs[groups + 2 :]
    cols, part, width = out[0].shape[1:]
    rows = first_ref.shape[0]
    half = rows // 2
    pitch, pitch_back = cols_pitch(spec_signal, cols), cols_pitch(mixed, rows)

    def forward(col, carry):
        field = jnp.concatenate(
            [jnp.concatenate([ref[which, col] for ref in fields], axis=0) for which in (1, 0)], axis=1
        )
        spec = dot(first_ref[...], jnp.concatenate([field, field], axis=0))
        place = pl.ds(pl.multiple_of(col * pitch, 8), rows)
        spec_signal[place, :] = spec[:, :width]
        spec_kernel[place, :] = spec[:, width:]
        return carry

    def middle(freq, edge):
        def take(row):
            place = pl.ds(row, cols, stride=pitch)
            return jnp.concatenate([spec_signal[place, :], spec_kernel[place, :]], axis=1)

        real = take(freq)
        imag = jnp.zeros_like(real) if edge else take(freq + half)
        spec = product(mid_ref[freq], jnp.concatenate([real, imag], axis=0))
        re_sig, im_sig = spec[:cols, :width], spec[cols:, :width]
        re_ker, im_ker = spec[:cols, width:], spec[cols:, width:]
        both = jnp.concatenate(
            [re_sig * re_ker - im_sig * im_ker, re_sig * im_ker + im_sig * re_ker], axis=0
        )
        field = product(back_ref[freq], both)
        mixed[pl.ds(pl.multiple_of(freq * pitch_back, 8), cols), :] = field[:cols]
        if not edge:
            place = pl.ds(pl.multiple_of((freq + half) * pitch_back, 8), cols)
            mixed[place, :] = field[cols:]

    def inner(freq, carry):
        middle(freq, False)
        return carry

    def backward(col, carry):
        field = mixed[pl.ds(col, rows, stride=pitch_back), :]
        result = product(last_ref[...], field).astype(jnp.bfloat16)
        for group in range(groups):
            slot_ref(out, group)[col] = result[group * part : (group + 1) * part]
        return carry

    lax.fori_loop(0, cols, forward, 0, unroll=16)
    middle(0, True)
    middle(half, True)
    lax.fori_loop(1, half, inner, 0, unroll=9 if (half - 1) % 9 == 0 else 1)
    lax.fori_loop(0, cols, backward, 0, unroll=16)


def cols_pitch(ref, count):
    return ref.shape[0] // count


def whole(shape):
    return pl.BlockSpec(shape, lambda *_: (0,) * len(shape))


def long_conv(me, fields):
    groups = len(fields)
    cols, part, width = fields[0][0].shape[2:]
    out = (groups // 2, cols, part, width)
    rows = 2 * groups * part
    first, mid, back, last = tables(rows, cols, groups)
    return pl.pallas_call(
        functools.partial(conv_kernel, groups),
        grid_spec=pltpu.PrefetchScalarGridSpec(
            num_scalar_prefetch=1,
            grid=(1,),
            in_specs=[
                pl.BlockSpec((None, *first.shape[1:]), lambda _, me: (me[0], 0, 0)),
                whole(mid.shape),
                whole(back.shape),
                pl.BlockSpec((None, *last.shape[1:]), lambda _, me: (me[0], 0, 0)),
            ]
            + [slot_spec(slot) for slot in fields],
            out_specs=[whole(out)] * 2,
            scratch_shapes=[pltpu.VMEM((cols * (rows + SPARE), width), jnp.float32)] * 2
            + [pltpu.VMEM((rows * (cols + SPARE), width), jnp.float32)],
        ),
        out_shape=[jax.ShapeDtypeStruct(out, jnp.bfloat16)] * 2,
        compiler_params=pltpu.CompilerParams(vmem_limit_bytes=VMEM_BYTES),
        cost_estimate=SHORT,
        name="long_conv",
    )(me, first, mid, back, last, *[array for array, _ in fields])


def spread(value, natural, out):
    cols, part, _ = out.shape
    pitch = cols + SPARE
    for slow in range(part):
        natural[slow * pitch : slow * pitch + cols, :] = value(slow * cols, cols)
    for col in range(cols):
        out[col] = natural[pl.ds(col, part, stride=pitch), :].astype(jnp.bfloat16)


def short_conv(buffer, stream, rim_ref, data_ref, taps_ref):
    count = data_ref.shape[0]
    taps = taps_ref.shape[1]
    buffer[SPARE - (taps - 1) : SPARE, :] = rim_ref[stream].astype(jnp.float32)
    buffer[SPARE : SPARE + count, :] = data_ref[...].astype(jnp.float32)

    def rows(begin, size):
        total = None
        for lag in range(taps):
            place = slice(SPARE + begin - lag, SPARE + begin - lag + size)
            term = taps_ref[stream, lag : lag + 1, :] * buffer[place, :]
            total = term if total is None else total + term
        return total

    return rows


def pieces_kernel(groups, me_ref, filter_ref, key_ref, value_ref, rim_ref, taps_ref, *refs):
    out, (natural, key_rows, value_rows) = refs[:2], refs[2:]
    key = short_conv(key_rows, 1, rim_ref, key_ref, taps_ref)
    value = short_conv(value_rows, 2, rim_ref, value_ref, taps_ref)
    for group in range(groups):

        @pl.when(pl.program_id(0) == group)
        def _(group=group):
            spread(
                lambda begin, size: filter_ref[begin : begin + size, :].astype(jnp.float32),
                natural,
                slot_ref(out, group).at[0],
            )
            spread(
                lambda begin, size: key(begin, size) * value(begin, size),
                natural,
                slot_ref(out, group).at[1],
            )


def gate_kernel(gate_ref, key_ref, value_ref, rim_ref, taps_ref, skip_ref, gating_ref, direct_ref, *rows):
    convs = [
        short_conv(buffer, stream, rim_ref, data, taps_ref)
        for stream, (buffer, data) in enumerate(zip(rows, (gate_ref, key_ref, value_ref)))
    ]
    step = 128
    for begin in range(0, gate_ref.shape[0], step):
        gating, key, value = (conv(begin, step) for conv in convs)
        mixed = (key * value).astype(jnp.bfloat16).astype(jnp.float32)
        gating_ref[begin : begin + step, :] = gating
        direct_ref[begin : begin + step, :] = skip_ref[...] * mixed


def gated_kernel(groups, me_ref, gating_ref, direct_ref, *refs):
    parts, (out, natural) = refs[:groups], refs[groups:]
    cols, part, _ = parts[0].shape
    pitch = cols + SPARE
    for group in range(groups):

        @pl.when(pl.program_id(0) == group)
        def _(group=group):
            for col in range(cols):
                natural[pl.ds(col, part, stride=pitch), :] = parts[group][col].astype(jnp.float32)

    for slow in range(part):
        place = slice(slow * cols, (slow + 1) * cols)
        long = natural[slow * pitch : slow * pitch + cols, :]
        out[place, :] = ((long + direct_ref[place, :]) * gating_ref[place, :]).astype(jnp.bfloat16)


def in_groups(kernel, groups, chunk, me, specs, out_specs, out_shape, scratch, name, *args):
    return pl.pallas_call(
        kernel,
        grid_spec=pltpu.PrefetchScalarGridSpec(
            num_scalar_prefetch=1,
            grid=(groups,),
            in_specs=specs,
            out_specs=out_specs,
            scratch_shapes=scratch,
        ),
        out_shape=out_shape,
        compiler_params=pltpu.CompilerParams(vmem_limit_bytes=VMEM_BYTES),
        cost_estimate=SHORT,
        name=name,
    )(me, *args)


class Chunk:
    def __init__(self, index, groups, tokens, me):
        self.groups, self.tokens, self.me = groups, tokens, me
        self.cols = tokens // PART
        self.piece = (self.cols, PART, LANES)
        self.block = lambda step, me: index * groups + (me[0] ^ step)
        self.index = index

    def column(self, *lead):
        sizes, places = zip(*lead)
        return pl.BlockSpec(
            (*sizes, LANES), lambda step, me: (*places, self.block(step, me))
        )

    def call(self, kernel, specs, out_specs, out_shape, scratch, name, *args):
        return in_groups(
            functools.partial(kernel, self.groups), self.groups, self.index, self.me,
            specs, out_specs, out_shape, scratch, name, *args,
        )

    def natural(self):
        return pltpu.VMEM((PART * (self.cols + SPARE), LANES), jnp.float32)

    def rows(self):
        return pltpu.VMEM((SPARE + self.tokens, LANES), jnp.float32)

    def pieces(self, long_filter, streams, rim, taps):
        specs = [self.column((self.tokens, 0))]
        specs += [self.column((None, stream), (self.tokens, 0)) for stream in (1, 2)]
        size = (self.groups // 2, 2, *self.piece)
        return self.call(
            pieces_kernel, specs + self.small(rim, taps), [whole(size)] * 2,
            [jax.ShapeDtypeStruct(size, jnp.bfloat16)] * 2,
            [self.natural(), self.rows(), self.rows()], "pieces", long_filter, streams, streams, rim, taps,
        )

    def small(self, rim, taps):
        return [
            self.column((rim.shape[0], 0), (rim.shape[1], 0)),
            self.column((taps.shape[0], 0), (taps.shape[1], 0)),
        ]

    def gates(self, streams, rim, taps, skip):
        specs = [self.column((None, stream), (self.tokens, 0)) for stream in range(3)]
        specs += self.small(rim, taps) + [self.column((1, 0))]
        spec = pl.BlockSpec((self.tokens, LANES), lambda step, me: (0, me[0] ^ step))
        shape = jax.ShapeDtypeStruct((self.tokens, self.groups * LANES), jnp.float32)

        def kernel(groups, me_ref, *refs):
            gate_kernel(*refs)

        return self.call(
            kernel, specs, [spec] * 2, [shape] * 2, [self.rows()] * 3, "gates",
            streams, streams, streams, rim, taps, skip,
        )

    def gated(self, gating, direct, parts):
        spec = pl.BlockSpec((self.tokens, LANES), lambda step, me: (0, me[0] ^ step))
        shape = jax.ShapeDtypeStruct((self.tokens, self.groups * LANES), jnp.bfloat16)
        return self.call(
            gated_kernel, [spec] * 2 + [slot_spec(slot) for slot in parts], spec, shape,
            [self.natural()], "gated", gating, direct, *[array for array, _ in parts],
        )


def ordered(bit, own, other):
    return jnp.where(bit == 0, own, other), jnp.where(bit == 0, other, own)


class Weights:
    def __init__(self, out_weight, chunks):
        self.whole, self.chunks = out_weight, chunks
        self.me, self.ctx = lax.axis_index("tp"), lax.axis_index("ctx")
        self.rows = out_weight.shape[0]
        self.width = out_weight.shape[1] // lax.axis_size("tp")

    def pair(self, high, other, begin, rows, source=None):
        block = ((self.me ^ (4 * high) ^ other) >> 1) * 2
        source = self.whole if source is None else source
        return lax.dynamic_slice(source, (begin, block * self.width), (rows, 2 * self.width))

    def own(self, high, low, *others):
        wanted = self.me ^ (4 * high + low)
        source = after(self.whole, *others)
        block = lax.dynamic_slice_in_dim(source, wanted * self.width, self.width, axis=1)
        return self.in_chunks(block)

    def in_chunks(self, block):
        step = self.rows // self.chunks
        return [block[i * step : (i + 1) * step] for i in range(self.chunks)]

    def sent(self, high, parts, source=None):
        rows = self.rows // parts
        return self.pair(high, 2, (self.ctx & (parts - 1)) * rows, rows, source)

    def low_block(self, pair, low):
        return lax.dynamic_slice_in_dim(pair, ((self.me & 1) ^ low) * self.width, self.width, axis=1)

    def joined(self, low, *pairs):
        core, chip = self.ctx & 1, (self.ctx >> 1) & 1
        pairs = [self.low_block(pair, low) for pair in pairs]
        parts = ordered(core, *pairs[:2])
        if len(pairs) == 4:
            chips = ordered(
                chip, jnp.concatenate(parts, 0), jnp.concatenate(ordered(core, *pairs[2:]), 0)
            )
            parts = chips
        if self.chunks == 2:
            return list(parts)
        return self.in_chunks(jnp.concatenate(parts, axis=0))


def widened(value, groups):
    group = value.shape[-1] // groups
    if group >= LANES:
        return value
    split = value.reshape(*value.shape[:-1], groups, group)
    padded = jnp.pad(split, [(0, 0)] * (split.ndim - 1) + [(0, LANES - group)])
    return padded.reshape(*value.shape[:-1], groups * LANES)


def on_device(streams, conv_weight, skip_weight, long_filter, out_weight):
    tokens, channels = streams.shape[1:]
    taps = conv_weight.shape[1]
    groups = lax.axis_size("ctx")
    me = lax.axis_index("ctx").astype(jnp.int32).reshape(1)
    group = channels // groups
    streams, conv_weight, skip_weight, long_filter = (
        widened(value, groups) for value in (streams, conv_weight, skip_weight[None], long_filter)
    )
    chunks = streams.shape[2] // (groups * LANES)
    rim = shifted(streams[:, tokens - (taps - 1) :, :], "ctx", 1)
    parts = [Chunk(index, groups, tokens, me) for index in range(chunks)]
    weights = Weights(out_weight, chunks)
    highs = range(lax.axis_size("tp") // 4)
    lows = range(2)

    sent = weights.sent(0, 4)
    near_direct = swapped(sent, "tp", 2)
    pieces = [parts[0].pieces(after(long_filter, sent), streams, rim, conv_weight)]
    own = {(high, low): weights.own(high, low, *pieces[0]) for high in highs for low in lows}
    settled = after(rim, *pieces[0], *[value for block in own.values() for value in block])
    gates = [part.gates(streams, settled, conv_weight, skip_weight) for part in parts]
    settled, *early = lax.optimization_barrier((settled, *[value for gate in gates for value in gate]))
    gates = [early[2 * index : 2 * index + 2] for index in range(chunks)]
    pieces += [part.pieces(long_filter, streams, settled, conv_weight) for part in parts[1:]]

    back = []
    sent = jnp.concatenate([weights.sent(high, 2) for high in reversed(highs) if high])
    direct = swapped(after(sent, near_direct), "tp", 2)
    field = exchanged(*pieces[0], settled, near_direct, *[value for piece in pieces[1:] for value in piece])
    for index, part in enumerate(parts):
        if index + 1 < chunks:
            low, high = pieces[index + 1]
            high = after(high, field[-1][0])
        result = long_conv(me, field)
        if index + 1 < chunks:
            field = exchanged(low, high, *result)
        back.append(result)
    results = back

    back, gated, blocks = [], [], {}
    for index, (part, gate, result) in enumerate(zip(parts, gates, results)):
        last = index == chunks - 1
        back.append(exchanged(*result, *(gated[-1:] if last else results[index + 1])))
        value = back[-1]
        if last:
            direct = after(direct, *gated[-1:], *results[-1])
            shared = swapped(direct, "ctx", 1)
            count = out_weight.shape[0] // 4
            near_direct = after(near_direct, *gated[-1:], *results[-1])
            nearest = (near_direct, swapped(near_direct, "ctx", 1))
            tie = []
            for high in highs:
                for low in lows:
                    if high:
                        place = slice(2 * count * (len(highs) - 1 - high), 2 * count * (len(highs) - high))
                        block = weights.joined(low, direct[place], shared[place])
                        blocks[high, low] = own[high, low] + block
                        tie += block
            value = tied(value, *tie)
        rows = part.gated(*gate, value)
        if group < LANES:
            rows = rows.reshape(tokens, groups, LANES)[:, :, :group].reshape(tokens, channels)
        gated.append(rows)
    crossed = swapped(after(nearest[0], gated[-1]), "ctx", 2)
    crossed = (crossed, swapped(crossed, "ctx", 1))
    for low in lows:
        blocks[0, low] = own[0, low] + weights.joined(low, *nearest, *crossed)
    return project(gated, blocks)


def project(gated, blocks):
    high_count = lax.axis_size("tp") // 4
    step = gated[0].shape[0] // PIECES
    cut = lambda value: [value[i * step : (i + 1) * step] for i in range(PIECES)]
    near = [cut(value) for value in gated]
    far = [cut(swapped(value, "tp", 2)) for value in gated[:-1]]
    far.append([swapped(value, "tp", 2) for value in near[-1]])
    values = [
        list(lax.optimization_barrier(tuple(value[piece] for value in near + far)))
        for piece in range(PIECES)
    ]

    def partial_sum(piece, high, low, *earlier):
        total = None
        for value, weight in zip(values[piece], blocks[high, low]):
            term = dot(after(value, *earlier), weight)
            total = term if total is None else total + term
        return total

    totals = {}
    arrived = [[] for _ in range(PIECES)]
    crossed = None
    for high in reversed(range(high_count)):
        earlier = [(value,) for value in crossed] if crossed else [()] * PIECES
        crossed = [
            swapped(partial_sum(piece, high, 1, *earlier[piece]).astype(jnp.bfloat16), "tp", 1)
            for piece in range(PIECES)
        ]
        for piece in range(PIECES):
            total = partial_sum(piece, high, 0) + crossed[piece].astype(jnp.float32)
            if high:
                arrived[piece].append(swapped(total.astype(jnp.bfloat16), "tp", 4 * high))
            else:
                totals[piece] = total
    results = []
    for piece in range(PIECES):
        total = totals[piece]
        for value in arrived[piece]:
            total = total + value.astype(jnp.float32)
        results.append(total.astype(jnp.bfloat16))
    return jnp.concatenate(results, axis=0)


PIECES = 4


def solution(mesh):
    return jax.shard_map(
        on_device,
        mesh=mesh,
        in_specs=(
            P(None, "ctx", "tp"),
            P(None, None, "tp"),
            P("tp"),
            P("ctx", "tp"),
            P("tp", None),
        ),
        out_specs=P("ctx", "tp"),
        check_vma=False,
    )
```

```python
import functools

import jax
import jax.numpy as jnp
import ml_dtypes
import numpy as np
from jax import lax
from jax.experimental import pallas as pl
from jax.experimental.pallas import tpu as pltpu
from jax.sharding import PartitionSpec as P

LANES = 128
PART = 16
SPARE = 8
VMEM_BYTES = 48 << 20
SHORT = pl.CostEstimate(flops=1, bytes_accessed=1, transcendentals=0)


def swapped(value, axis, bits):
    count = lax.axis_size(axis)
    return lax.ppermute(value, axis, [(source, source ^ bits) for source in range(count)])


def shifted(value, axis, steps):
    count = lax.axis_size(axis)
    initial, last = (max(0, -steps), min(count, count - steps))
    return lax.ppermute(value, axis, [(source, source + steps) for source in range(initial, last)])


def after(value, *others):
    return lax.optimization_barrier((value, *others))[0]


def exchanged(low, high, *others):
    half = low.shape[0]
    high = after(swapped(high, "ctx", half), *others)
    slots = [(low, place) for place in range(half)] + [(high, place) for place in range(half)]
    bit = half // 2
    while bit:
        moving = [slot for slot in range(2 * half) if slot & bit]
        sent = jnp.stack([slots[slot][0][slots[slot][1]] for slot in moving])
        arrived = swapped(sent, "ctx", bit)
        for place, slot in enumerate(moving):
            slots[slot] = (arrived, place)
        bit //= 2
    return slots


def slot_spec(slot):
    array, place = slot
    return pl.BlockSpec((None, *array.shape[1:]), lambda *_: (place,) + (0,) * (array.ndim - 1))


def slot_ref(halves, slot):
    count = halves[0].shape[0]
    return halves[slot // count].at[slot % count]


def tied(slots, *others):
    array, place = slots[0]
    return [(after(array, *others), place)] + slots[1:]


def tables(rows, cols, groups):
    half = rows // 2
    total = rows * cols
    slow, freq = np.arange(half), np.arange(half + 1)
    angle = 2 * np.pi * (freq[:, None] * slow[None, :] % rows) / rows
    first = np.concatenate([np.cos(angle), -np.sin(angle)[1:half]], 0)
    weight = np.where((freq == 0) | (freq == half), 1.0, 2.0)[:, None] / total
    last = np.concatenate([np.cos(angle) * weight, -(np.sin(angle) * weight)[1:half]], 0).T
    order = (np.arange(groups)[:, None] ^ np.arange(groups)[None, :])[:, :, None] * (half // groups)
    order = (order + np.arange(half // groups)).reshape(groups, half)
    col = np.arange(cols)
    turn = rows * col[None, :, None] * col[None, None, :]
    angle = 2 * np.pi * ((freq[:, None, None] * col[None, None, :] + turn) % total) / total
    cosine, sine = np.cos(angle), np.sin(angle)
    middle = np.concatenate(
        [np.concatenate([cosine, sine], 2), np.concatenate([-sine, cosine], 2)], 1
    )

    def pair(value):
        high = value.astype(ml_dtypes.bfloat16)
        low = (value - high.astype(np.float64)).astype(ml_dtypes.bfloat16)
        return np.concatenate([high, low], -1)

    first_all = np.stack([pair(first[:, own]) for own in order])
    last_all = np.stack([pair(last[own]) for own in order])
    return first_all, pair(middle), pair(middle.transpose(0, 2, 1)), last_all


def dot(left, right):
    return jnp.dot(left, right, preferred_element_type=jnp.float32)


def product(table, value):
    high = value.astype(jnp.bfloat16)
    low = (value - high.astype(jnp.float32)).astype(jnp.bfloat16)
    return dot(
        jnp.concatenate([table, table], axis=1), jnp.concatenate([high, high, low, low], axis=0)
    )


def conv_kernel(groups, me_ref, first_ref, mid_ref, back_ref, last_ref, *refs):
    fields, out = refs[:groups], refs[groups : groups + 2]
    spec_signal, spec_kernel, mixed = refs[groups + 2 :]
    cols, part, width = out[0].shape[1:]
    rows = first_ref.shape[0]
    half = rows // 2
    pitch, pitch_back = cols_pitch(spec_signal, cols), cols_pitch(mixed, rows)

    def forward(col, carry):
        field = jnp.concatenate(
            [jnp.concatenate([ref[which, col] for ref in fields], axis=0) for which in (1, 0)], axis=1
        )
        spec = dot(first_ref[...], jnp.concatenate([field, field], axis=0))
        place = pl.ds(pl.multiple_of(col * pitch, 8), rows)
        spec_signal[place, :] = spec[:, :width]
        spec_kernel[place, :] = spec[:, width:]
        return carry

    def middle(freq, edge):
        def take(row):
            place = pl.ds(row, cols, stride=pitch)
            return jnp.concatenate([spec_signal[place, :], spec_kernel[place, :]], axis=1)

        real = take(freq)
        imag = jnp.zeros_like(real) if edge else take(freq + half)
        spec = product(mid_ref[freq], jnp.concatenate([real, imag], axis=0))
        re_sig, im_sig = spec[:cols, :width], spec[cols:, :width]
        re_ker, im_ker = spec[:cols, width:], spec[cols:, width:]
        both = jnp.concatenate(
            [re_sig * re_ker - im_sig * im_ker, re_sig * im_ker + im_sig * re_ker], axis=0
        )
        field = product(back_ref[freq], both)
        mixed[pl.ds(pl.multiple_of(freq * pitch_back, 8), cols), :] = field[:cols]
        if not edge:
            place = pl.ds(pl.multiple_of((freq + half) * pitch_back, 8), cols)
            mixed[place, :] = field[cols:]

    def inner(freq, carry):
        middle(freq, False)
        return carry

    def backward(col, carry):
        field = mixed[pl.ds(col, rows, stride=pitch_back), :]
        result = product(last_ref[...], field).astype(jnp.bfloat16)
        for group in range(groups):
            slot_ref(out, group)[col] = result[group * part : (group + 1) * part]
        return carry

    lax.fori_loop(0, cols, forward, 0, unroll=16)
    middle(0, True)
    middle(half, True)
    lax.fori_loop(1, half, inner, 0, unroll=9 if (half - 1) % 9 == 0 else 1)
    lax.fori_loop(0, cols, backward, 0, unroll=16)


def cols_pitch(ref, count):
    return ref.shape[0] // count


def whole(shape):
    return pl.BlockSpec(shape, lambda *_: (0,) * len(shape))


def long_conv(me, fields):
    groups = len(fields)
    cols, part, width = fields[0][0].shape[2:]
    out = (groups // 2, cols, part, width)
    rows = 2 * groups * part
    first, mid, back, last = tables(rows, cols, groups)
    return pl.pallas_call(
        functools.partial(conv_kernel, groups),
        grid_spec=pltpu.PrefetchScalarGridSpec(
            num_scalar_prefetch=1,
            grid=(1,),
            in_specs=[
                pl.BlockSpec((None, *first.shape[1:]), lambda _, me: (me[0], 0, 0)),
                whole(mid.shape),
                whole(back.shape),
                pl.BlockSpec((None, *last.shape[1:]), lambda _, me: (me[0], 0, 0)),
            ]
            + [slot_spec(slot) for slot in fields],
            out_specs=[whole(out)] * 2,
            scratch_shapes=[pltpu.VMEM((cols * (rows + SPARE), width), jnp.float32)] * 2
            + [pltpu.VMEM((rows * (cols + SPARE), width), jnp.float32)],
        ),
        out_shape=[jax.ShapeDtypeStruct(out, jnp.bfloat16)] * 2,
        compiler_params=pltpu.CompilerParams(vmem_limit_bytes=VMEM_BYTES),
        cost_estimate=SHORT,
        name="long_conv",
    )(me, first, mid, back, last, *[array for array, _ in fields])


def spread(value, natural, out):
    cols, part, _ = out.shape
    pitch = cols + SPARE
    for slow in range(part):
        natural[slow * pitch : slow * pitch + cols, :] = value(slow * cols, cols)
    for col in range(cols):
        out[col] = natural[pl.ds(col, part, stride=pitch), :].astype(jnp.bfloat16)


def short_conv(buffer, stream, rim_ref, data_ref, taps_ref):
    count = data_ref.shape[0]
    taps = taps_ref.shape[1]
    buffer[SPARE - (taps - 1) : SPARE, :] = rim_ref[stream].astype(jnp.float32)
    buffer[SPARE : SPARE + count, :] = data_ref[...].astype(jnp.float32)

    def rows(begin, size):
        total = None
        for lag in range(taps):
            place = slice(SPARE + begin - lag, SPARE + begin - lag + size)
            term = taps_ref[stream, lag : lag + 1, :] * buffer[place, :]
            total = term if total is None else total + term
        return total

    return rows


def pieces_kernel(groups, me_ref, filter_ref, key_ref, value_ref, rim_ref, taps_ref, *refs):
    out, (natural, key_rows, value_rows) = refs[:2], refs[2:]
    key = short_conv(key_rows, 1, rim_ref, key_ref, taps_ref)
    value = short_conv(value_rows, 2, rim_ref, value_ref, taps_ref)
    for group in range(groups):

        @pl.when(pl.program_id(0) == group)
        def _(group=group):
            spread(
                lambda begin, size: filter_ref[begin : begin + size, :].astype(jnp.float32),
                natural,
                slot_ref(out, group).at[0],
            )
            spread(
                lambda begin, size: key(begin, size) * value(begin, size),
                natural,
                slot_ref(out, group).at[1],
            )


def gate_kernel(gate_ref, key_ref, value_ref, rim_ref, taps_ref, skip_ref, gating_ref, direct_ref, *rows):
    convs = [
        short_conv(buffer, stream, rim_ref, data, taps_ref)
        for stream, (buffer, data) in enumerate(zip(rows, (gate_ref, key_ref, value_ref)))
    ]
    step = 128
    for begin in range(0, gate_ref.shape[0], step):
        gating, key, value = (conv(begin, step) for conv in convs)
        mixed = (key * value).astype(jnp.bfloat16).astype(jnp.float32)
        gating_ref[begin : begin + step, :] = gating
        direct_ref[begin : begin + step, :] = skip_ref[...] * mixed


def gated_kernel(groups, me_ref, gating_ref, direct_ref, *refs):
    parts, (out, natural) = refs[:groups], refs[groups:]
    cols, part, _ = parts[0].shape
    pitch = cols + SPARE
    for group in range(groups):

        @pl.when(pl.program_id(0) == group)
        def _(group=group):
            for col in range(cols):
                natural[pl.ds(col, part, stride=pitch), :] = parts[group][col].astype(jnp.float32)

    for slow in range(part):
        place = slice(slow * cols, (slow + 1) * cols)
        long = natural[slow * pitch : slow * pitch + cols, :]
        out[place, :] = ((long + direct_ref[place, :]) * gating_ref[place, :]).astype(jnp.bfloat16)


def in_groups(kernel, groups, chunk, me, specs, out_specs, out_shape, scratch, name, *args):
    return pl.pallas_call(
        kernel,
        grid_spec=pltpu.PrefetchScalarGridSpec(
            num_scalar_prefetch=1,
            grid=(groups,),
            in_specs=specs,
            out_specs=out_specs,
            scratch_shapes=scratch,
        ),
        out_shape=out_shape,
        compiler_params=pltpu.CompilerParams(vmem_limit_bytes=VMEM_BYTES),
        cost_estimate=SHORT,
        name=name,
    )(me, *args)


class Chunk:
    def __init__(self, index, groups, tokens, me):
        self.groups, self.tokens, self.me = groups, tokens, me
        self.cols = tokens // PART
        self.piece = (self.cols, PART, LANES)
        self.block = lambda step, me: index * groups + (me[0] ^ step)
        self.index = index

    def column(self, *lead):
        sizes, places = zip(*lead)
        return pl.BlockSpec(
            (*sizes, LANES), lambda step, me: (*places, self.block(step, me))
        )

    def call(self, kernel, specs, out_specs, out_shape, scratch, name, *args):
        return in_groups(
            functools.partial(kernel, self.groups), self.groups, self.index, self.me,
            specs, out_specs, out_shape, scratch, name, *args,
        )

    def natural(self):
        return pltpu.VMEM((PART * (self.cols + SPARE), LANES), jnp.float32)

    def rows(self):
        return pltpu.VMEM((SPARE + self.tokens, LANES), jnp.float32)

    def pieces(self, long_filter, streams, rim, taps):
        specs = [self.column((self.tokens, 0))]
        specs += [self.column((None, stream), (self.tokens, 0)) for stream in (1, 2)]
        size = (self.groups // 2, 2, *self.piece)
        return self.call(
            pieces_kernel, specs + self.small(rim, taps), [whole(size)] * 2,
            [jax.ShapeDtypeStruct(size, jnp.bfloat16)] * 2,
            [self.natural(), self.rows(), self.rows()], "pieces", long_filter, streams, streams, rim, taps,
        )

    def small(self, rim, taps):
        return [
            self.column((rim.shape[0], 0), (rim.shape[1], 0)),
            self.column((taps.shape[0], 0), (taps.shape[1], 0)),
        ]

    def gates(self, streams, rim, taps, skip):
        specs = [self.column((None, stream), (self.tokens, 0)) for stream in range(3)]
        specs += self.small(rim, taps) + [self.column((1, 0))]
        spec = pl.BlockSpec((self.tokens, LANES), lambda step, me: (0, me[0] ^ step))
        shape = jax.ShapeDtypeStruct((self.tokens, self.groups * LANES), jnp.float32)

        def kernel(groups, me_ref, *refs):
            gate_kernel(*refs)

        return self.call(
            kernel, specs, [spec] * 2, [shape] * 2, [self.rows()] * 3, "gates",
            streams, streams, streams, rim, taps, skip,
        )

    def gated(self, gating, direct, parts):
        spec = pl.BlockSpec((self.tokens, LANES), lambda step, me: (0, me[0] ^ step))
        shape = jax.ShapeDtypeStruct((self.tokens, self.groups * LANES), jnp.bfloat16)
        return self.call(
            gated_kernel, [spec] * 2 + [slot_spec(slot) for slot in parts], spec, shape,
            [self.natural()], "gated", gating, direct, *[array for array, _ in parts],
        )


def ordered(bit, own, other):
    return jnp.where(bit == 0, own, other), jnp.where(bit == 0, other, own)


class Weights:
    def __init__(self, out_weight, chunks):
        self.whole, self.chunks = out_weight, chunks
        self.me, self.ctx = lax.axis_index("tp"), lax.axis_index("ctx")
        self.rows = out_weight.shape[0]
        self.width = out_weight.shape[1] // lax.axis_size("tp")

    def pair(self, high, other, begin, rows, source=None):
        block = ((self.me ^ (4 * high) ^ other) >> 1) * 2
        source = self.whole if source is None else source
        return lax.dynamic_slice(source, (begin, block * self.width), (rows, 2 * self.width))

    def own(self, high, low, *others):
        wanted = self.me ^ (4 * high + low)
        source = after(self.whole, *others)
        block = lax.dynamic_slice_in_dim(source, wanted * self.width, self.width, axis=1)
        return self.in_chunks(block)

    def in_chunks(self, block):
        step = self.rows // self.chunks
        return [block[i * step : (i + 1) * step] for i in range(self.chunks)]

    def sent(self, high, parts, source=None):
        rows = self.rows // parts
        return self.pair(high, 2, (self.ctx & (parts - 1)) * rows, rows, source)

    def low_block(self, pair, low):
        return lax.dynamic_slice_in_dim(pair, ((self.me & 1) ^ low) * self.width, self.width, axis=1)

    def joined(self, low, *pairs):
        core, chip = self.ctx & 1, (self.ctx >> 1) & 1
        pairs = [self.low_block(pair, low) for pair in pairs]
        parts = ordered(core, *pairs[:2])
        if len(pairs) == 4:
            chips = ordered(
                chip, jnp.concatenate(parts, 0), jnp.concatenate(ordered(core, *pairs[2:]), 0)
            )
            parts = chips
        if self.chunks == 2:
            return list(parts)
        return self.in_chunks(jnp.concatenate(parts, axis=0))


def widened(value, groups):
    group = value.shape[-1] // groups
    if group >= LANES:
        return value
    split = value.reshape(*value.shape[:-1], groups, group)
    padded = jnp.pad(split, [(0, 0)] * (split.ndim - 1) + [(0, LANES - group)])
    return padded.reshape(*value.shape[:-1], groups * LANES)


def on_device(streams, conv_weight, skip_weight, long_filter, out_weight):
    tokens, channels = streams.shape[1:]
    taps = conv_weight.shape[1]
    groups = lax.axis_size("ctx")
    me = lax.axis_index("ctx").astype(jnp.int32).reshape(1)
    group = channels // groups
    streams, conv_weight, skip_weight, long_filter = (
        widened(value, groups) for value in (streams, conv_weight, skip_weight[None], long_filter)
    )
    chunks = streams.shape[2] // (groups * LANES)
    rim = shifted(streams[:, tokens - (taps - 1) :, :], "ctx", 1)
    parts = [Chunk(index, groups, tokens, me) for index in range(chunks)]
    weights = Weights(out_weight, chunks)
    highs = range(lax.axis_size("tp") // 4)
    lows = range(2)

    sent = weights.sent(0, 4)
    near_direct = swapped(sent, "tp", 2)
    pieces = [parts[0].pieces(after(long_filter, sent), streams, rim, conv_weight)]
    own = {(high, low): weights.own(high, low, *pieces[0]) for high in highs for low in lows}
    settled = after(rim, *pieces[0], *[value for block in own.values() for value in block])
    gates = [part.gates(streams, settled, conv_weight, skip_weight) for part in parts]
    settled, *early = lax.optimization_barrier((settled, *[value for gate in gates for value in gate]))
    gates = [early[2 * index : 2 * index + 2] for index in range(chunks)]
    pieces += [part.pieces(long_filter, streams, settled, conv_weight) for part in parts[1:]]

    back = []
    sent = jnp.concatenate([weights.sent(high, 2) for high in reversed(highs) if high])
    direct = swapped(after(sent, near_direct), "tp", 2)
    field = exchanged(*pieces[0], settled, near_direct, *[value for piece in pieces[1:] for value in piece])
    for index, part in enumerate(parts):
        if index + 1 < chunks:
            low, high = pieces[index + 1]
            high = after(high, field[-1][0])
        result = long_conv(me, field)
        if index + 1 < chunks:
            field = exchanged(low, high, *result)
        back.append(result)
    results = back

    back, gated, blocks = [], [], {}
    for index, (part, gate, result) in enumerate(zip(parts, gates, results)):
        last = index == chunks - 1
        back.append(exchanged(*result, *(gated[-1:] if last else results[index + 1])))
        value = back[-1]
        if last:
            direct = after(direct, *gated[-1:], *results[-1])
            shared = swapped(direct, "ctx", 1)
            count = out_weight.shape[0] // 4
            near_direct = after(near_direct, *gated[-1:], *results[-1])
            nearest = (near_direct, swapped(near_direct, "ctx", 1))
            tie = []
            for high in highs:
                for low in lows:
                    if high:
                        place = slice(2 * count * (len(highs) - 1 - high), 2 * count * (len(highs) - high))
                        block = weights.joined(low, direct[place], shared[place])
                        blocks[high, low] = own[high, low] + block
                        tie += block
            value = tied(value, *tie)
        rows = part.gated(*gate, value)
        if group < LANES:
            rows = rows.reshape(tokens, groups, LANES)[:, :, :group].reshape(tokens, channels)
        gated.append(rows)
    crossed = swapped(after(nearest[0], gated[-1]), "ctx", 2)
    crossed = (crossed, swapped(crossed, "ctx", 1))
    for low in lows:
        blocks[0, low] = own[0, low] + weights.joined(low, *nearest, *crossed)
    return project(gated, blocks)


def project(gated, blocks):
    high_count = lax.axis_size("tp") // 4
    step = gated[0].shape[0] // PIECES
    cut = lambda value: [value[i * step : (i + 1) * step] for i in range(PIECES)]
    near = [cut(value) for value in gated]
    far = [cut(swapped(value, "tp", 2)) for value in gated[:-1]]
    far.append([swapped(value, "tp", 2) for value in near[-1]])
    values, sums = [], []

    def collect(piece):
        rows = [value[piece] for value in near + far]
        values.append(list(lax.optimization_barrier((*rows, *sums[-1:])))[: len(rows)])

    def partial_sum(piece, high, low, *earlier):
        total = None
        for value, weight in zip(values[piece], blocks[high, low]):
            term = dot(after(value, *earlier), weight)
            total = term if total is None else total + term
        return total

    totals = {}
    arrived = [[] for _ in range(PIECES)]
    crossed = None
    for high in reversed(range(high_count)):
        earlier = [(value,) for value in crossed] if crossed else [()] * PIECES
        crossed = []
        for piece in range(PIECES):
            if len(values) < PIECES:
                collect(piece)
            sums.append(partial_sum(piece, high, 1, *earlier[piece]).astype(jnp.bfloat16))
            crossed.append(swapped(sums[-1], "tp", 1))
        for piece in range(PIECES):
            total = partial_sum(piece, high, 0) + crossed[piece].astype(jnp.float32)
            if high:
                arrived[piece].append(swapped(total.astype(jnp.bfloat16), "tp", 4 * high))
            else:
                totals[piece] = total
    results = []
    for piece in range(PIECES):
        total = totals[piece]
        for value in arrived[piece]:
            total = total + value.astype(jnp.float32)
        results.append(total.astype(jnp.bfloat16))
    return jnp.concatenate(results, axis=0)


PIECES = 4


def solution(mesh):
    return jax.shard_map(
        on_device,
        mesh=mesh,
        in_specs=(
            P(None, "ctx", "tp"),
            P(None, None, "tp"),
            P("tp"),
            P("ctx", "tp"),
            P("tp", None),
        ),
        out_specs=P("ctx", "tp"),
        check_vma=False,
    )
```

```python
import functools

import jax
import jax.numpy as jnp
import ml_dtypes
import numpy as np
from jax import lax
from jax.experimental import pallas as pl
from jax.experimental.pallas import tpu as pltpu
from jax.sharding import PartitionSpec as P

LANES = 128
PART = 16
SPARE = 8
VMEM_BYTES = 48 << 20
SHORT = pl.CostEstimate(flops=1, bytes_accessed=1, transcendentals=0)


def swapped(value, axis, bits):
    count = lax.axis_size(axis)
    return lax.ppermute(value, axis, [(source, source ^ bits) for source in range(count)])


def shifted(value, axis, steps):
    count = lax.axis_size(axis)
    initial, last = (max(0, -steps), min(count, count - steps))
    return lax.ppermute(value, axis, [(source, source + steps) for source in range(initial, last)])


def after(value, *others):
    return lax.optimization_barrier((value, *others))[0]


def exchanged(low, high, *others):
    half = low.shape[0]
    high = after(swapped(high, "ctx", half), *others)
    slots = [(low, place) for place in range(half)] + [(high, place) for place in range(half)]
    bit = half // 2
    while bit:
        moving = [slot for slot in range(2 * half) if slot & bit]
        sent = jnp.stack([slots[slot][0][slots[slot][1]] for slot in moving])
        arrived = swapped(sent, "ctx", bit)
        for place, slot in enumerate(moving):
            slots[slot] = (arrived, place)
        bit //= 2
    return slots


def slot_spec(slot):
    array, place = slot
    return pl.BlockSpec((None, *array.shape[1:]), lambda *_: (place,) + (0,) * (array.ndim - 1))


def slot_ref(halves, slot):
    count = halves[0].shape[0]
    return halves[slot // count].at[slot % count]


def tied(slots, *others):
    array, place = slots[0]
    return [(after(array, *others), place)] + slots[1:]


def tables(rows, cols, groups):
    half = rows // 2
    total = rows * cols
    slow, freq = np.arange(half), np.arange(half + 1)
    angle = 2 * np.pi * (freq[:, None] * slow[None, :] % rows) / rows
    first = np.concatenate([np.cos(angle), -np.sin(angle)[1:half]], 0)
    weight = np.where((freq == 0) | (freq == half), 1.0, 2.0)[:, None] / total
    last = np.concatenate([np.cos(angle) * weight, -(np.sin(angle) * weight)[1:half]], 0).T
    order = (np.arange(groups)[:, None] ^ np.arange(groups)[None, :])[:, :, None] * (half // groups)
    order = (order + np.arange(half // groups)).reshape(groups, half)
    col = np.arange(cols)
    turn = rows * col[None, :, None] * col[None, None, :]
    angle = 2 * np.pi * ((freq[:, None, None] * col[None, None, :] + turn) % total) / total
    cosine, sine = np.cos(angle), np.sin(angle)
    middle = np.concatenate(
        [np.concatenate([cosine, sine], 2), np.concatenate([-sine, cosine], 2)], 1
    )

    def pair(value):
        high = value.astype(ml_dtypes.bfloat16)
        low = (value - high.astype(np.float64)).astype(ml_dtypes.bfloat16)
        return np.concatenate([high, low], -1)

    first_all = np.stack([pair(first[:, own]) for own in order])
    last_all = np.stack([pair(last[own]) for own in order])
    return first_all, pair(middle), pair(middle.transpose(0, 2, 1)), last_all


def dot(left, right):
    return jnp.dot(left, right, preferred_element_type=jnp.float32)


def product(table, value):
    high = value.astype(jnp.bfloat16)
    low = (value - high.astype(jnp.float32)).astype(jnp.bfloat16)
    return dot(
        jnp.concatenate([table, table], axis=1), jnp.concatenate([high, high, low, low], axis=0)
    )


def conv_kernel(groups, me_ref, first_ref, mid_ref, back_ref, last_ref, *refs):
    fields, out = refs[:groups], refs[groups : groups + 2]
    spec_signal, spec_kernel, mixed = refs[groups + 2 :]
    cols, part, width = out[0].shape[1:]
    rows = first_ref.shape[0]
    half = rows // 2
    pitch, pitch_back = cols_pitch(spec_signal, cols), cols_pitch(mixed, rows)

    def forward(col, carry):
        field = jnp.concatenate(
            [jnp.concatenate([ref[which, col] for ref in fields], axis=0) for which in (1, 0)], axis=1
        )
        spec = dot(first_ref[...], jnp.concatenate([field, field], axis=0))
        place = pl.ds(pl.multiple_of(col * pitch, 8), rows)
        spec_signal[place, :] = spec[:, :width]
        spec_kernel[place, :] = spec[:, width:]
        return carry

    def middle(freq, edge):
        def take(row):
            place = pl.ds(row, cols, stride=pitch)
            return jnp.concatenate([spec_signal[place, :], spec_kernel[place, :]], axis=1)

        real = take(freq)
        imag = jnp.zeros_like(real) if edge else take(freq + half)
        spec = product(mid_ref[freq], jnp.concatenate([real, imag], axis=0))
        re_sig, im_sig = spec[:cols, :width], spec[cols:, :width]
        re_ker, im_ker = spec[:cols, width:], spec[cols:, width:]
        both = jnp.concatenate(
            [re_sig * re_ker - im_sig * im_ker, re_sig * im_ker + im_sig * re_ker], axis=0
        )
        field = product(back_ref[freq], both)
        mixed[pl.ds(pl.multiple_of(freq * pitch_back, 8), cols), :] = field[:cols]
        if not edge:
            place = pl.ds(pl.multiple_of((freq + half) * pitch_back, 8), cols)
            mixed[place, :] = field[cols:]

    def inner(freq, carry):
        middle(freq, False)
        return carry

    def backward(col, carry):
        field = mixed[pl.ds(col, rows, stride=pitch_back), :]
        result = product(last_ref[...], field).astype(jnp.bfloat16)
        for group in range(groups):
            slot_ref(out, group)[col] = result[group * part : (group + 1) * part]
        return carry

    lax.fori_loop(0, cols, forward, 0, unroll=16)
    middle(0, True)
    middle(half, True)
    lax.fori_loop(1, half, inner, 0, unroll=9 if (half - 1) % 9 == 0 else 1)
    lax.fori_loop(0, cols, backward, 0, unroll=16)


def cols_pitch(ref, count):
    return ref.shape[0] // count


def whole(shape):
    return pl.BlockSpec(shape, lambda *_: (0,) * len(shape))


def long_conv(me, fields):
    groups = len(fields)
    cols, part, width = fields[0][0].shape[2:]
    out = (groups // 2, cols, part, width)
    rows = 2 * groups * part
    first, mid, back, last = tables(rows, cols, groups)
    return pl.pallas_call(
        functools.partial(conv_kernel, groups),
        grid_spec=pltpu.PrefetchScalarGridSpec(
            num_scalar_prefetch=1,
            grid=(1,),
            in_specs=[
                pl.BlockSpec((None, *first.shape[1:]), lambda _, me: (me[0], 0, 0)),
                whole(mid.shape),
                whole(back.shape),
                pl.BlockSpec((None, *last.shape[1:]), lambda _, me: (me[0], 0, 0)),
            ]
            + [slot_spec(slot) for slot in fields],
            out_specs=[whole(out)] * 2,
            scratch_shapes=[pltpu.VMEM((cols * (rows + SPARE), width), jnp.float32)] * 2
            + [pltpu.VMEM((rows * (cols + SPARE), width), jnp.float32)],
        ),
        out_shape=[jax.ShapeDtypeStruct(out, jnp.bfloat16)] * 2,
        compiler_params=pltpu.CompilerParams(vmem_limit_bytes=VMEM_BYTES),
        cost_estimate=SHORT,
        name="long_conv",
    )(me, first, mid, back, last, *[array for array, _ in fields])


def spread(value, natural, out):
    cols, part, _ = out.shape
    pitch = cols + SPARE
    for slow in range(part):
        natural[slow * pitch : slow * pitch + cols, :] = value(slow * cols, cols)
    for col in range(cols):
        out[col] = natural[pl.ds(col, part, stride=pitch), :].astype(jnp.bfloat16)


def short_conv(buffer, stream, rim_ref, data_ref, taps_ref):
    count = data_ref.shape[0]
    taps = taps_ref.shape[1]
    buffer[SPARE - (taps - 1) : SPARE, :] = rim_ref[stream].astype(jnp.float32)
    buffer[SPARE : SPARE + count, :] = data_ref[...].astype(jnp.float32)

    def rows(begin, size):
        total = None
        for lag in range(taps):
            place = slice(SPARE + begin - lag, SPARE + begin - lag + size)
            term = taps_ref[stream, lag : lag + 1, :] * buffer[place, :]
            total = term if total is None else total + term
        return total

    return rows


def pieces_kernel(groups, me_ref, filter_ref, key_ref, value_ref, rim_ref, taps_ref, *refs):
    out, (natural, key_rows, value_rows) = refs[:2], refs[2:]
    key = short_conv(key_rows, 1, rim_ref, key_ref, taps_ref)
    value = short_conv(value_rows, 2, rim_ref, value_ref, taps_ref)
    for group in range(groups):

        @pl.when(pl.program_id(0) == group)
        def _(group=group):
            spread(
                lambda begin, size: filter_ref[begin : begin + size, :].astype(jnp.float32),
                natural,
                slot_ref(out, group).at[0],
            )
            spread(
                lambda begin, size: key(begin, size) * value(begin, size),
                natural,
                slot_ref(out, group).at[1],
            )


def gate_kernel(gate_ref, key_ref, value_ref, rim_ref, taps_ref, skip_ref, gating_ref, direct_ref, *rows):
    convs = [
        short_conv(buffer, stream, rim_ref, data, taps_ref)
        for stream, (buffer, data) in enumerate(zip(rows, (gate_ref, key_ref, value_ref)))
    ]
    step = 128
    for begin in range(0, gate_ref.shape[0], step):
        gating, key, value = (conv(begin, step) for conv in convs)
        mixed = (key * value).astype(jnp.bfloat16).astype(jnp.float32)
        gating_ref[begin : begin + step, :] = gating
        direct_ref[begin : begin + step, :] = skip_ref[...] * mixed


def gated_kernel(groups, me_ref, gating_ref, direct_ref, *refs):
    parts, (out, natural) = refs[:groups], refs[groups:]
    cols, part, _ = parts[0].shape
    pitch = cols + SPARE
    for group in range(groups):

        @pl.when(pl.program_id(0) == group)
        def _(group=group):
            for col in range(cols):
                natural[pl.ds(col, part, stride=pitch), :] = parts[group][col].astype(jnp.float32)

    for slow in range(part):
        place = slice(slow * cols, (slow + 1) * cols)
        long = natural[slow * pitch : slow * pitch + cols, :]
        out[place, :] = ((long + direct_ref[place, :]) * gating_ref[place, :]).astype(jnp.bfloat16)


def in_groups(kernel, groups, chunk, me, specs, out_specs, out_shape, scratch, name, *args):
    return pl.pallas_call(
        kernel,
        grid_spec=pltpu.PrefetchScalarGridSpec(
            num_scalar_prefetch=1,
            grid=(groups,),
            in_specs=specs,
            out_specs=out_specs,
            scratch_shapes=scratch,
        ),
        out_shape=out_shape,
        compiler_params=pltpu.CompilerParams(vmem_limit_bytes=VMEM_BYTES),
        cost_estimate=SHORT,
        name=name,
    )(me, *args)


class Chunk:
    def __init__(self, index, groups, tokens, me):
        self.groups, self.tokens, self.me = groups, tokens, me
        self.cols = tokens // PART
        self.piece = (self.cols, PART, LANES)
        self.block = lambda step, me: index * groups + (me[0] ^ step)
        self.index = index

    def column(self, *lead):
        sizes, places = zip(*lead)
        return pl.BlockSpec(
            (*sizes, LANES), lambda step, me: (*places, self.block(step, me))
        )

    def call(self, kernel, specs, out_specs, out_shape, scratch, name, *args):
        return in_groups(
            functools.partial(kernel, self.groups), self.groups, self.index, self.me,
            specs, out_specs, out_shape, scratch, name, *args,
        )

    def natural(self):
        return pltpu.VMEM((PART * (self.cols + SPARE), LANES), jnp.float32)

    def rows(self):
        return pltpu.VMEM((SPARE + self.tokens, LANES), jnp.float32)

    def pieces(self, long_filter, streams, rim, taps):
        specs = [self.column((self.tokens, 0))]
        specs += [self.column((None, stream), (self.tokens, 0)) for stream in (1, 2)]
        size = (self.groups // 2, 2, *self.piece)
        return self.call(
            pieces_kernel, specs + self.small(rim, taps), [whole(size)] * 2,
            [jax.ShapeDtypeStruct(size, jnp.bfloat16)] * 2,
            [self.natural(), self.rows(), self.rows()], "pieces", long_filter, streams, streams, rim, taps,
        )

    def small(self, rim, taps):
        return [
            self.column((rim.shape[0], 0), (rim.shape[1], 0)),
            self.column((taps.shape[0], 0), (taps.shape[1], 0)),
        ]

    def gates(self, streams, rim, taps, skip):
        specs = [self.column((None, stream), (self.tokens, 0)) for stream in range(3)]
        specs += self.small(rim, taps) + [self.column((1, 0))]
        spec = pl.BlockSpec((self.tokens, LANES), lambda step, me: (0, me[0] ^ step))
        shape = jax.ShapeDtypeStruct((self.tokens, self.groups * LANES), jnp.float32)

        def kernel(groups, me_ref, *refs):
            gate_kernel(*refs)

        return self.call(
            kernel, specs, [spec] * 2, [shape] * 2, [self.rows()] * 3, "gates",
            streams, streams, streams, rim, taps, skip,
        )

    def gated(self, gating, direct, parts):
        spec = pl.BlockSpec((self.tokens, LANES), lambda step, me: (0, me[0] ^ step))
        shape = jax.ShapeDtypeStruct((self.tokens, self.groups * LANES), jnp.bfloat16)
        return self.call(
            gated_kernel, [spec] * 2 + [slot_spec(slot) for slot in parts], spec, shape,
            [self.natural()], "gated", gating, direct, *[array for array, _ in parts],
        )


def ordered(bit, own, other):
    return jnp.where(bit == 0, own, other), jnp.where(bit == 0, other, own)


class Weights:
    def __init__(self, out_weight, chunks):
        self.whole, self.chunks = out_weight, chunks
        self.me, self.ctx = lax.axis_index("tp"), lax.axis_index("ctx")
        self.rows = out_weight.shape[0]
        self.width = out_weight.shape[1] // lax.axis_size("tp")

    def pair(self, high, other, begin, rows, source=None):
        block = ((self.me ^ (4 * high) ^ other) >> 1) * 2
        source = self.whole if source is None else source
        return lax.dynamic_slice(source, (begin, block * self.width), (rows, 2 * self.width))

    def own(self, high, low, *others):
        wanted = self.me ^ (4 * high + low)
        source = after(self.whole, *others)
        block = lax.dynamic_slice_in_dim(source, wanted * self.width, self.width, axis=1)
        return self.in_chunks(block)

    def in_chunks(self, block):
        step = self.rows // self.chunks
        return [block[i * step : (i + 1) * step] for i in range(self.chunks)]

    def sent(self, high, parts, source=None):
        rows = self.rows // parts
        return self.pair(high, 2, (self.ctx & (parts - 1)) * rows, rows, source)

    def low_block(self, pair, low):
        return lax.dynamic_slice_in_dim(pair, ((self.me & 1) ^ low) * self.width, self.width, axis=1)

    def joined(self, low, *pairs):
        core, chip = self.ctx & 1, (self.ctx >> 1) & 1
        pairs = [self.low_block(pair, low) for pair in pairs]
        parts = ordered(core, *pairs[:2])
        if len(pairs) == 4:
            chips = ordered(
                chip, jnp.concatenate(parts, 0), jnp.concatenate(ordered(core, *pairs[2:]), 0)
            )
            parts = chips
        if self.chunks == 2:
            return list(parts)
        return self.in_chunks(jnp.concatenate(parts, axis=0))


def widened(value, groups):
    group = value.shape[-1] // groups
    if group >= LANES:
        return value
    split = value.reshape(*value.shape[:-1], groups, group)
    padded = jnp.pad(split, [(0, 0)] * (split.ndim - 1) + [(0, LANES - group)])
    return padded.reshape(*value.shape[:-1], groups * LANES)


def on_device(streams, conv_weight, skip_weight, long_filter, out_weight):
    tokens, channels = streams.shape[1:]
    taps = conv_weight.shape[1]
    groups = lax.axis_size("ctx")
    me = lax.axis_index("ctx").astype(jnp.int32).reshape(1)
    group = channels // groups
    streams, conv_weight, skip_weight, long_filter = (
        widened(value, groups) for value in (streams, conv_weight, skip_weight[None], long_filter)
    )
    chunks = streams.shape[2] // (groups * LANES)
    rim = shifted(streams[:, tokens - (taps - 1) :, :], "ctx", 1)
    parts = [Chunk(index, groups, tokens, me) for index in range(chunks)]
    weights = Weights(out_weight, chunks)
    highs = range(lax.axis_size("tp") // 4)
    lows = range(2)

    sent = weights.sent(0, 4)
    near_direct = swapped(sent, "tp", 2)
    pieces = [parts[0].pieces(after(long_filter, sent), streams, rim, conv_weight)]
    own = {(high, low): weights.own(high, low, *pieces[0]) for high in highs for low in lows}
    settled = after(rim, *pieces[0], *[value for block in own.values() for value in block])
    gates = [part.gates(streams, settled, conv_weight, skip_weight) for part in parts]
    settled, *early = lax.optimization_barrier((settled, *[value for gate in gates for value in gate]))
    gates = [early[2 * index : 2 * index + 2] for index in range(chunks)]
    pieces += [part.pieces(long_filter, streams, settled, conv_weight) for part in parts[1:]]

    back = []
    sent = jnp.concatenate([weights.sent(high, 2) for high in reversed(highs) if high])
    settled, sent = lax.optimization_barrier((settled, sent))
    direct = swapped(after(sent, near_direct), "tp", 2)
    field = exchanged(*pieces[0], settled, near_direct, *[value for piece in pieces[1:] for value in piece])
    for index, part in enumerate(parts):
        if index + 1 < chunks:
            low, high = pieces[index + 1]
            high = after(high, field[groups // 2][0])
        result = long_conv(me, field)
        if index + 1 < chunks:
            field = exchanged(low, high, *result)
        back.append(result)
    results = back

    back, gated, blocks = [], [], {}
    for index, (part, gate, result) in enumerate(zip(parts, gates, results)):
        last = index == chunks - 1
        back.append(exchanged(*result, *(gated[-1:] if last else results[index + 1])))
        value = back[-1]
        if last:
            direct = after(direct, *gated[-1:], *results[-1])
            shared = swapped(direct, "ctx", 1)
            count = out_weight.shape[0] // 4
            near_direct = after(near_direct, *gated[-1:], *results[-1])
            nearest = (near_direct, swapped(near_direct, "ctx", 1))
            tie = []
            for high in highs:
                for low in lows:
                    if high:
                        place = slice(2 * count * (len(highs) - 1 - high), 2 * count * (len(highs) - high))
                        block = weights.joined(low, direct[place], shared[place])
                        blocks[high, low] = own[high, low] + block
                        tie += block
            value = tied(value, *tie)
        rows = part.gated(*gate, value)
        if group < LANES:
            rows = rows.reshape(tokens, groups, LANES)[:, :, :group].reshape(tokens, channels)
        gated.append(rows)
    crossed = swapped(after(nearest[0], gated[-1]), "ctx", 2)
    crossed = (crossed, swapped(crossed, "ctx", 1))
    for low in lows:
        blocks[0, low] = own[0, low] + weights.joined(low, *nearest, *crossed)
    return project(gated, blocks)


def project(gated, blocks):
    high_count = lax.axis_size("tp") // 4
    step = gated[0].shape[0] // PIECES
    cut = lambda value: [value[i * step : (i + 1) * step] for i in range(PIECES)]
    near = [cut(value) for value in gated]
    far = [cut(swapped(value, "tp", 2)) for value in gated[:-1]]
    far.append([swapped(value, "tp", 2) for value in near[-1]])
    values, sums = [], []

    def collect(piece):
        rows = [value[piece] for value in near + far]
        values.append(list(lax.optimization_barrier((*rows, *sums[-1:])))[: len(rows)])

    def partial_sum(piece, high, low, *earlier):
        total = None
        for value, weight in zip(values[piece], blocks[high, low]):
            term = dot(after(value, *earlier), weight)
            total = term if total is None else total + term
        return total

    totals = {}
    arrived = [[] for _ in range(PIECES)]
    crossed = None
    for high in reversed(range(high_count)):
        earlier = [(value,) for value in crossed] if crossed else [()] * PIECES
        crossed = []
        for piece in range(PIECES):
            if len(values) < PIECES:
                collect(piece)
            sums.append(partial_sum(piece, high, 1, *earlier[piece]).astype(jnp.bfloat16))
            crossed.append(swapped(sums[-1], "tp", 1))
        for piece in range(PIECES):
            total = partial_sum(piece, high, 0) + crossed[piece].astype(jnp.float32)
            if high:
                arrived[piece].append(swapped(total.astype(jnp.bfloat16), "tp", 4 * high))
            else:
                totals[piece] = total
    results = []
    for piece in range(PIECES):
        total = totals[piece]
        for value in arrived[piece]:
            total = total + value.astype(jnp.float32)
        results.append(total.astype(jnp.bfloat16))
    return jnp.concatenate(results, axis=0)


PIECES = 4


def solution(mesh):
    return jax.shard_map(
        on_device,
        mesh=mesh,
        in_specs=(
            P(None, "ctx", "tp"),
            P(None, None, "tp"),
            P("tp"),
            P("ctx", "tp"),
            P("tp", None),
        ),
        out_specs=P("ctx", "tp"),
        check_vma=False,
    )
```
